256 devices in a mesh: row: 16 (over z, core), col: 16 (over x, y).
Axes of the slice: x: 4, y: 4, z: 8, core: 2. Of those that a mesh axis runs over, the one named last changes fastest.
Arguments:
- acts: bfloat16 [512, 16384], P('col', 'row'), may hold values from -6 to 6
- gate_weight: bfloat16 [16384, 26624], P('row', 'col'), may hold values from -0.046875 to 0.046875
- up_weight: bfloat16 [16384, 26624], P('row', 'col'), may hold values from -0.046875 to 0.046875
- down_weight: bfloat16 [26624, 16384], P('col', 'row'), may hold values from -0.0390625 to 0.0390625
Outputs:
- block_out: bfloat16 [512, 16384], P('col', 'row')
The draws below stay inside these ranges and needn't reach their ends.
All inputs are finite; a program needn't handle non-finite values.
Results may differ from the reference program's by a relative error of at most 0.019.
Values may be sent and summed in bfloat16 or wider, within the bound.
No kernel may reach another device: no remote copies, remote signals or barrier semaphores. Data moves between devices by JAX's collectives and lax.ppermute only.
A program may use at most 64 MiB of HBM per device.

```python
import jax
import jax.numpy as jnp

D = 16384
FF = 26624
TOKENS = 512


def steps_of(rng, shape, cuts, low, top_value):
    loudness, own = 1.0, jax.random.fold_in(rng, 6)
    for position, parts in cuts:
        heights = jnp.exp(jax.random.uniform(jax.random.fold_in(own, position), (parts,), jnp.float32, low / len(cuts), top_value / len(cuts)))
        loudness = loudness * jnp.repeat(heights, shape[position] // parts).reshape([-1 if axis == position else 1 for axis in range(len(shape))])
    return loudness


def gaussian(own_key, extent, deviation, bound, cuts=(), held_as=jnp.bfloat16):
    result = deviation * jax.random.normal(own_key, extent, jnp.float32)
    if cuts:
        result = result * steps_of(own_key, extent, cuts, -0.22, 0.18)
    return jnp.clip(result, -bound, bound).astype(held_as)


def setup_inputs(seed: int = 0) -> dict:
    key_list = jax.random.split(jax.random.key(seed), 5)
    return {
        "acts": gaussian(key_list[0], (TOKENS, D), 1.0, 6.0, ((0, 16), (1, 16))),
        "gate_weight": gaussian(key_list[1], (D, FF), D ** -0.5, 0.046875, ((0, 16), (1, 16))),
        "up_weight": gaussian(key_list[2], (D, FF), D ** -0.5, 0.046875, ((0, 16), (1, 16))),
        "down_weight": gaussian(key_list[3], (FF, D), FF ** -0.5, 0.0390625, ((0, 16), (1, 16))),
    }


def reference(acts, gate_weight, up_weight, down_weight):
    gate = jnp.dot(acts, gate_weight, preferred_element_type=jnp.float32)
    up = jnp.dot(acts, up_weight, preferred_element_type=jnp.float32)
    hidden = (jax.nn.silu(gate) * up).astype(jnp.bfloat16)
    return jnp.dot(hidden, down_weight, preferred_element_type=jnp.float32).astype(jnp.bfloat16)
```

```python
import jax
import jax.numpy as jnp
from jax import lax
from jax.sharding import Mesh, PartitionSpec as P

BF = jnp.bfloat16
F32 = jnp.float32


def shift(v, axis, n, s):
    return lax.ppermute(v, axis, [(i, (i + s) % n) for i in range(n)])


def block(x, i):
    return lax.dynamic_index_in_dim(x, i, 0, keepdims=False)


def gather_near(v, axis, n):
    return jnp.concatenate([v] + [shift(v, axis, n, s) for s in range(1, n)], 0)


def unrotate(v, axis, n):
    me = lax.axis_index(axis)
    v = jnp.flip(v, 0)
    return jnp.roll(v, me + 1, 0)


def reduce_ring(x, axis, n):
    me, h, c = lax.axis_index(axis), n // 2, x.shape[2]
    cut = c // 256 * 128
    far = block(x, (me + h) % n)
    right, left = shift(far[:, :cut], axis, n, 1), shift(far[:, cut:], axis, n, -1)
    for k in range(h - 1, 0, -1):
        ours_r, ours_l = block(x, (me + k) % n), block(x, (me - k) % n)
        if k == h - 1:
            right = jnp.concatenate([ours_r[:, :cut] + right, ours_r[:, cut:]], 1)
            left = jnp.concatenate([ours_l[:, :cut], ours_l[:, cut:] + left], 1)
        else:
            right, left = ours_r + right, ours_l + left
        right, left = shift(right, axis, n, 1), shift(left, axis, n, -1)
    return block(x, me).astype(F32) + right.astype(F32) + left.astype(F32)


def on_device(acts, gate_weight, up_weight, down_weight):
    width = gate_weight.shape[1]
    nz, nx, ny = lax.axis_size("z"), lax.axis_size("x"), lax.axis_size("y")
    core = lax.axis_index("core")
    piece = gather_near(acts, "x", nx).reshape(nx, -1, acts.shape[1])
    piece = unrotate(piece, "x", nx).reshape(-1, acts.shape[1])
    piece = gather_near(piece, "y", ny).reshape(ny, nx, -1, acts.shape[1])
    piece = unrotate(piece, "y", ny).swapaxes(0, 1).reshape(-1, acts.shape[1])
    half = piece.shape[0] // 2

    def both(rows):
        return jnp.concatenate(
            [jnp.dot(rows, w, preferred_element_type=F32) for w in (gate_weight, up_weight)], 1
        )

    theirs = both(lax.dynamic_slice_in_dim(piece, (1 - core) * half, half)).astype(BF)
    theirs = shift(theirs, "core", 2, 1)
    ours = both(lax.dynamic_slice_in_dim(piece, core * half, half))
    ours = (ours + theirs.astype(F32)).astype(BF).reshape(nz, half // nz, 2 * width)
    summed = reduce_ring(ours, "z", nz)
    hidden = (jax.nn.silu(summed[:, :width]) * summed[:, width:]).astype(BF)
    hidden = gather_near(hidden, "z", nz).reshape(nz, -1, width)
    hidden = unrotate(hidden, "z", nz).reshape(half, width)
    other = shift(hidden, "core", 2, 1)
    low = jnp.where(core == 0, hidden, other)
    high = jnp.where(core == 0, other, hidden)
    terms = jnp.dot(jnp.concatenate([low, high], 0), down_weight, preferred_element_type=F32)
    terms = terms.astype(BF).reshape(nx * ny, -1, down_weight.shape[1])
    terms = lax.all_to_all(terms, ("x", "y"), 0, 0, tiled=True)
    return jnp.sum(terms.astype(F32), 0).astype(BF)


def solution(mesh):
    grid = Mesh(mesh.devices.reshape(8, 2, 4, 4), ("z", "core", "x", "y"))
    row, col = ("z", "core"), ("x", "y")
    in_specs = (P(col, row), P(row, col), P(row, col), P(col, row))
    return jax.shard_map(
        on_device, mesh=grid, in_specs=in_specs, out_specs=P(col, row), check_vma=False
    )
```

```python
import jax
import jax.numpy as jnp
from jax import lax
from jax.experimental import pallas as pl
from jax.experimental.pallas import tpu as pltpu
from jax.sharding import Mesh, PartitionSpec as P

BF = jnp.bfloat16
F32 = jnp.float32
VMEM = pl.BlockSpec(memory_space=pltpu.VMEM)
ANY = pl.BlockSpec(memory_space=pl.ANY)
MIB = 2**20

OWNER = (0, 3, 4, 7, 1, 6, 2, 5)
POSITION = sum(t << (4 * z) for t, z in enumerate(OWNER))
STEPS = (1, -1, 3)


def partner(z, step):
    return (z + STEPS[step] * (1 - 2 * (z % 2)) + 8) % 8


def swap_z(v, step):
    pairs = []
    for z in range(8):
        pairs.append((2 * z, 2 * partner(z, step)))
        pairs.append((2 * z + 1, 2 * ((8 - partner((8 - z) % 8, step)) % 8) + 1))
    return lax.ppermute(v, ("z", "core"), pairs)


def swap_core(v):
    return lax.ppermute(v, "core", [(0, 1), (1, 0)])


def swap_grid(v, near, far):
    pairs = []
    for x in range(4):
        for y in range(4):
            pairs.append((4 * x + y, 4 * (x ^ near) + (y ^ far)))
            pairs.append((16 + 4 * x + y, 16 + 4 * (x ^ far) + (y ^ near)))
    return lax.ppermute(v, ("core", "x", "y"), pairs)


def own_z():
    z = lax.axis_index("z")
    return jnp.where(lax.axis_index("core") == 0, z, (8 - z) % 8)


def is_in(z, members):
    return ((sum(1 << m for m in members) >> z) & 1) == 1


def shape(*dims, dtype=BF):
    return jax.ShapeDtypeStruct(dims, dtype)


def call(body, outs, *ins, flops=0, specs=None, scratch=(), limit=16):
    size = sum(v.size * v.dtype.itemsize for v in (*ins, *outs))
    return pl.pallas_call(
        body,
        out_shape=outs,
        in_specs=specs or [VMEM] * len(ins),
        out_specs=[VMEM] * len(outs),
        scratch_shapes=list(scratch),
        cost_estimate=pl.CostEstimate(flops=flops, bytes_accessed=size, transcendentals=0),
        compiler_params=pltpu.CompilerParams(vmem_limit_bytes=limit * MIB),
    )(*ins)


def load(weight):
    def body(source, out, sem):
        copy = pltpu.make_async_copy(source, out, sem)
        copy.start()
        copy.wait()

    sems = [pltpu.SemaphoreType.DMA(())]
    return call(body, [shape(*weight.shape)], weight, specs=[ANY], scratch=sems, limit=48)[0]


def join(*parts):
    rows = [p.shape[0] for p in parts]

    def body(*refs):
        at = 0
        for ref, n in zip(refs, rows):
            refs[-1][at : at + n] = ref[...]
            at += n

    return call(body, [shape(sum(rows), *parts[0].shape[1:])], *parts)[0]


def tiles(width, tile):
    return [(at, min(tile, width - at)) for at in range(0, width, tile)]


def project(part, first, second, gate_weight, up_weight, after=()):
    _, rows, depth = first.shape
    width = gate_weight.shape[1]
    half = 4 * rows

    def body(first, second, gate, up, *refs):
        theirs, ours, left = refs[len(after) :]
        mine = 2 * (part ^ lax.axis_index("core"))
        for j, ref in enumerate((first, second)):
            for h in range(2):
                at = (2 * j + h) * rows
                left[at : at + rows] = ref[2 - mine + h]
                left[half + at : half + at + rows] = ref[mine + h]
        for at, n in tiles(width, 256):
            for i, weight in enumerate((gate, up)):
                out = jnp.dot(left[...], weight[:, at : at + n], preferred_element_type=F32).astype(BF)
                theirs[:, i, :, at : at + n] = out[:half].reshape(4, rows, n)
                ours[:, i, :, at : at + n] = out[half:].reshape(4, rows, n)

    return call(
        body, [shape(4, 2, rows, width)] * 2, first, second, gate_weight, up_weight, *after,
        specs=[VMEM] * 4 + [ANY] * len(after), flops=8 * half * depth * width, scratch=[pltpu.VMEM((2 * half, depth), BF)],
    )


def first_sums(ours, theirs):
    _, _, rows, width = ours[0].shape

    def body(o0, o1, t0, t1, send, keep):
        core = lax.axis_index("core")

        def total(t, i):
            p, j, k = t // 4, t // 2 % 2, t % 2
            o, r, s = ((o0, t0, t1), (o1, t1, t0))[p]
            got = jnp.where(core == 0, r[2 * k + j, i], s[2 * k + j, i])
            return o[t % 4, i].astype(F32) + got.astype(F32)

        def fill(kept, sent):
            for n in range(4):
                for i in range(2):
                    send[n, i] = total(sent + n, i).astype(BF)
                    keep[n, i] = total(kept + n, i)

        inside = is_in(own_z(), OWNER[:4])
        pl.when(inside)(lambda: fill(0, 4))
        pl.when(jnp.logical_not(inside))(lambda: fill(4, 0))

    outs = [shape(4, 2, rows, width), shape(4, 2, rows, width, dtype=F32)]
    return call(body, outs, *ours, *theirs)


def next_sums(got, kept, after=()):
    n, _, rows, width = got.shape
    m = n // 2
    firsts = OWNER[0:2] + OWNER[4:6] if m == 2 else OWNER[::2]

    def body(got, kept, *refs):
        send, keep = refs[len(after) :]
        at = jnp.where(is_in(own_z(), firsts), 0, m)
        for i in range(m):
            send[i] = (got[m - at + i].astype(F32) + kept[m - at + i]).astype(BF)
            keep[i] = got[at + i].astype(F32) + kept[at + i]

    outs = [shape(m, 2, rows, width), shape(m, 2, rows, width, dtype=F32)]
    return call(body, outs, got, kept, *after, specs=[VMEM] * 2 + [ANY] * len(after))


def activate(got, kept):
    _, _, rows, width = got.shape

    def body(got, kept, out):
        gate = got[0, 0].astype(F32) + kept[0, 0]
        up = got[0, 1].astype(F32) + kept[0, 1]
        out[0] = (gate / (1 + jnp.exp(-gate)) * up).astype(BF)

    return call(body, [shape(1, rows, width)], got, kept)[0]


def assemble(sent, got):
    _, rows, width = sent.shape

    def body(sent, got, out):
        me = own_z()
        for source, ref in ((me, sent), (partner(me, 0), got)):
            near = partner(source, 1)
            for i, owner in enumerate((source, partner(source, 2), near, partner(near, 2))):
                out[(POSITION >> (4 * owner)) & 7] = ref[i]

    return call(body, [shape(8, rows, width)], sent, got)[0]


def expand(own, other, weight):
    _, rows, depth = own.shape
    columns = weight.shape[1]

    def body(own, other, weight, *refs):
        outs, left = refs[:4], refs[4]
        core = lax.axis_index("core")
        for j in range(4):
            for q in range(4):
                at = (4 * j + q) * rows
                if q < 2:
                    left[at : at + rows] = own[2 * j + q]
                else:
                    left[at : at + rows] = other[4 * ((j >> 1) ^ 1 ^ core) + 2 * (q - 2) + (j & 1)]
        for at, n in tiles(columns, 256):
            out = jnp.dot(left[...], weight[:, at : at + n], preferred_element_type=F32).astype(BF)
            out = out.reshape(4, 4, rows, n)
            for j in range(4):
                outs[j][:, :, at : at + n] = out[j]

    return call(
        body, [shape(4, rows, columns)] * 4, own, other, weight,
        flops=32 * rows * depth * columns, scratch=[pltpu.VMEM((16 * rows, depth), BF)],
    )


def sum_far(*parts):
    _, rows, columns = parts[0].shape

    def body(a, b, c, d, keep, *sends):
        core = lax.axis_index("core")
        for k in range(4):
            low, high = k ^ (2 * core), k ^ 2 ^ (2 * core)
            total = (a[low].astype(F32) + b[low].astype(F32)) + (c[high].astype(F32) + d[high].astype(F32))
            if k == 0:
                keep[...] = total
            else:
                sends[k - 1][...] = total.astype(BF)

    outs = [shape(rows, columns, dtype=F32)] + [shape(rows, columns)] * 3
    return call(body, outs, *parts)


def sum_near(*parts):
    def body(a, b, c, d, out):
        total = (a[...] + b[...].astype(F32)) + (c[...].astype(F32) + d[...].astype(F32))
        out[...] = total.astype(BF)

    return call(body, [shape(*parts[0].shape)], *parts)[0]


def on_device(acts, gate_weight, up_weight, down_weight):
    own = acts[None]
    near = [swap_grid(own, k, 0) for k in (1, 2, 3)]
    gate_weight = load(gate_weight)
    piece = join(load(own), *near)
    far = [swap_grid(piece, 0, j) for j in (1, 2, 3)]
    up_weight = load(up_weight)
    theirs0, ours0 = project(0, piece, far[0], gate_weight, up_weight)
    theirs1, ours1 = project(1, far[1], far[2], gate_weight, up_weight, after=(theirs0,))
    send, keep = first_sums((ours0, ours1), (swap_core(theirs0), swap_core(theirs1)))
    down_weight = load(down_weight)
    send, keep = next_sums(swap_z(send, 0), keep, after=(down_weight,))
    send, keep = next_sums(swap_z(send, 1), keep)
    have = activate(swap_z(send, 2), keep)
    for step in (2, 1):
        have = join(have, swap_z(have, step))
    hidden = assemble(have, swap_z(have, 0))
    terms = expand(hidden, swap_core(hidden), down_weight)
    sums = sum_far(terms[0], *[swap_grid(terms[j], 0, j) for j in (1, 2, 3)])
    return sum_near(sums[0], *[swap_grid(sums[k], k, 0) for k in (1, 2, 3)])


def solution(mesh):
    grid = Mesh(mesh.devices.reshape(8, 2, 4, 4), ("z", "core", "x", "y"))
    row, col = ("z", "core"), ("x", "y")
    in_specs = (P(col, row), P(row, col), P(row, col), P(col, row))
    return jax.shard_map(
        on_device, mesh=grid, in_specs=in_specs, out_specs=P(col, row), check_vma=False
    )
```

```python
import jax
import jax.numpy as jnp
from jax import lax
from jax.experimental import pallas as pl
from jax.experimental.pallas import tpu as pltpu
from jax.sharding import Mesh, PartitionSpec as P

BF = jnp.bfloat16
F32 = jnp.float32
VMEM = pl.BlockSpec(memory_space=pltpu.VMEM)
ANY = pl.BlockSpec(memory_space=pl.ANY)
MIB = 2**20

OWNER = (0, 3, 4, 7, 1, 6, 2, 5)
POSITION = sum(t << (4 * z) for t, z in enumerate(OWNER))
STEPS = (1, -1, 3)


def partner(z, step):
    return (z + STEPS[step] * (1 - 2 * (z % 2)) + 8) % 8


def swap_z(v, step):
    pairs = []
    for z in range(8):
        pairs.append((2 * z, 2 * partner(z, step)))
        pairs.append((2 * z + 1, 2 * ((8 - partner((8 - z) % 8, step)) % 8) + 1))
    return lax.ppermute(v, ("z", "core"), pairs)


def swap_core(v):
    return lax.ppermute(v, "core", [(0, 1), (1, 0)])


def swap_grid(v, near, far):
    pairs = []
    for x in range(4):
        for y in range(4):
            pairs.append((4 * x + y, 4 * (x ^ near) + (y ^ far)))
            pairs.append((16 + 4 * x + y, 16 + 4 * (x ^ far) + (y ^ near)))
    return lax.ppermute(v, ("core", "x", "y"), pairs)


def own_z():
    z = lax.axis_index("z")
    return jnp.where(lax.axis_index("core") == 0, z, (8 - z) % 8)


def is_in(z, members):
    return ((sum(1 << m for m in members) >> z) & 1) == 1


def shape(*dims, dtype=BF):
    return jax.ShapeDtypeStruct(dims, dtype)


def call(body, outs, *ins, flops=0, spec=VMEM, scratch=(), limit=16, after=()):
    size = sum(v.size * v.dtype.itemsize for v in (*ins, *outs))
    n = len(ins)
    return pl.pallas_call(
        lambda *refs: body(*refs[len(after) :]),
        out_shape=outs,
        in_specs=[ANY] * len(after) + [spec] * n,
        out_specs=[VMEM] * len(outs),
        scratch_shapes=list(scratch),
        cost_estimate=pl.CostEstimate(flops=1, bytes_accessed=1, transcendentals=0),
        compiler_params=pltpu.CompilerParams(vmem_limit_bytes=limit * MIB),
    )(*after, *ins)


def load(weight):
    def body(source, out, sem):
        copy = pltpu.make_async_copy(source, out, sem)
        copy.start()
        copy.wait()

    sems = [pltpu.SemaphoreType.DMA(())]
    return call(body, [shape(*weight.shape)], weight, spec=ANY, scratch=sems, limit=48)[0]


def join(*parts, after=()):
    rows = [p.shape[0] for p in parts]

    def body(*refs):
        at = 0
        for ref, n in zip(refs, rows):
            refs[-1][at : at + n] = ref[...]
            at += n

    return call(body, [shape(sum(rows), *parts[0].shape[1:])], *parts, after=after)[0]


def tiles(start, stop, tile):
    return [(at, min(tile, stop - at)) for at in range(start, stop, tile)]


def project(part, columns, first, second, gate_weight, up_weight, after=()):
    _, rows, depth = first.shape
    half = 4 * rows
    widths = [stop - start for start, stop in columns]

    def body(first, second, gate, up, *refs):
        left = refs[-1]
        mine = 2 * (part ^ lax.axis_index("core"))
        for j, ref in enumerate((first, second)):
            for h in range(2):
                at = (2 * j + h) * rows
                left[at : at + rows] = ref[2 - mine + h]
                left[half + at : half + at + rows] = ref[mine + h]
        for n, (start, stop) in enumerate(columns):
            theirs, ours = refs[2 * n : 2 * n + 2]
            for at, size in tiles(start, stop, 256):
                to = slice(at - start, at - start + size)
                for i, weight in enumerate((gate, up)):
                    out = jnp.dot(left[...], weight[:, at : at + size], preferred_element_type=F32)
                    out = out.astype(BF)
                    theirs[:, i, :, to] = out[:half].reshape(4, rows, size)
                    ours[:, i, :, to] = out[half:].reshape(4, rows, size)

    outs = [shape(4, 2, rows, width) for width in widths for _ in range(2)]
    return call(
        body, outs, first, second, gate_weight, up_weight,
        flops=8 * half * depth * sum(widths), scratch=[pltpu.VMEM((2 * half, depth), BF)], after=after,
    )


def first_sums(ours, theirs, after=()):
    _, _, rows, width = ours[0].shape

    def body(o0, o1, t0, t1, send, keep):
        core = lax.axis_index("core")

        def total(t, i):
            p, j, k = t // 4, t // 2 % 2, t % 2
            o, r, s = ((o0, t0, t1), (o1, t1, t0))[p]
            got = jnp.where(core == 0, r[2 * k + j, i], s[2 * k + j, i])
            return o[t % 4, i].astype(F32) + got.astype(F32)

        def fill(kept, sent):
            for n in range(4):
                for i in range(2):
                    send[n, i] = total(sent + n, i).astype(BF)
                    keep[n, i] = total(kept + n, i)

        inside = is_in(own_z(), OWNER[:4])
        pl.when(inside)(lambda: fill(0, 4))
        pl.when(jnp.logical_not(inside))(lambda: fill(4, 0))

    outs = [shape(4, 2, rows, width), shape(4, 2, rows, width, dtype=F32)]
    return call(body, outs, *ours, *theirs, after=after)


def next_sums(got, kept, after=()):
    n, _, rows, width = got.shape
    m = n // 2
    firsts = OWNER[0:2] + OWNER[4:6] if m == 2 else OWNER[::2]

    def body(got, kept, send, keep):
        at = jnp.where(is_in(own_z(), firsts), 0, m)
        for i in range(m):
            send[i] = (got[m - at + i].astype(F32) + kept[m - at + i]).astype(BF)
            keep[i] = got[at + i].astype(F32) + kept[at + i]

    outs = [shape(m, 2, rows, width), shape(m, 2, rows, width, dtype=F32)]
    return call(body, outs, got, kept, after=after)


def activate(got, kept, after=()):
    _, _, rows, width = got.shape

    def body(got, kept, out):
        gate = got[0, 0].astype(F32) + kept[0, 0]
        up = got[0, 1].astype(F32) + kept[0, 1]
        out[0] = (gate / (1 + jnp.exp(-gate)) * up).astype(BF)

    return call(body, [shape(1, rows, width)], got, kept, after=after)[0]


def assemble(sent, got, after=()):
    _, rows, width = sent.shape

    def body(sent, got, out):
        me = own_z()
        for source, ref in ((me, sent), (partner(me, 0), got)):
            near = partner(source, 1)
            for i, owner in enumerate((source, partner(source, 2), near, partner(near, 2))):
                out[(POSITION >> (4 * owner)) & 7] = ref[i]

    return call(body, [shape(8, rows, width)], sent, got, after=after)[0]


def order(own, other, left):
    rows = own.shape[1]
    core = lax.axis_index("core")
    for j in range(4):
        for q in range(4):
            at = (4 * j + q) * rows
            if q < 2:
                left[at : at + rows] = own[2 * j + q]
            else:
                left[at : at + rows] = other[4 * ((j >> 1) ^ 1 ^ core) + 2 * (q - 2) + (j & 1)]


def expand(own, other, weight):
    _, rows, depth = own.shape
    columns = weight.shape[1]

    def body(own, other, weight, total, left):
        order(own, other, left)
        for at, n in tiles(0, columns, 256):
            right = weight[:depth, at : at + n]
            total[:, at : at + n] = jnp.dot(left[...], right, preferred_element_type=F32)

    return call(
        body, [shape(16 * rows, columns, dtype=F32)], own, other, weight,
        flops=32 * rows * depth * columns, scratch=[pltpu.VMEM((16 * rows, depth), BF)],
    )[0]


def expand_rest(own, other, weight, total):
    _, rows, depth = own.shape
    columns = weight.shape[1]
    start = weight.shape[0] - depth

    def body(own, other, weight, total, *refs):
        outs, left = refs[:4], refs[4]
        order(own, other, left)
        for at, n in tiles(0, columns, 256):
            right = weight[start:, at : at + n]
            out = jnp.dot(left[...], right, preferred_element_type=F32) + total[:, at : at + n]
            out = out.astype(BF).reshape(4, 4, rows, n)
            for j in range(4):
                outs[j][:, :, at : at + n] = out[j]

    return call(
        body, [shape(4, rows, columns)] * 4, own, other, weight, total,
        flops=32 * rows * depth * columns, scratch=[pltpu.VMEM((16 * rows, depth), BF)],
    )


def sum_far(*parts):
    _, rows, columns = parts[0].shape

    def body(a, c, b, d, keep, *sends):
        core = lax.axis_index("core")
        for k in range(4):
            low, high = k ^ (2 * core), k ^ 2 ^ (2 * core)
            total = (a[low].astype(F32) + b[low].astype(F32)) + (c[high].astype(F32) + d[high].astype(F32))
            if k == 0:
                keep[...] = total
            else:
                sends[k - 1][...] = total.astype(BF)

    outs = [shape(rows, columns, dtype=F32)] + [shape(rows, columns)] * 3
    return call(body, outs, *parts)


def sum_near(*parts):
    def body(a, b, c, d, out):
        total = (a[...] + b[...].astype(F32)) + (c[...].astype(F32) + d[...].astype(F32))
        out[...] = total.astype(BF)

    return call(body, [shape(*parts[0].shape)], *parts)[0]


def on_device(acts, gate_weight, up_weight, down_weight):
    own = acts[None]
    near = [swap_grid(own, k, 0) for k in (1, 2, 3)]
    gate_weight = load(gate_weight)
    piece = join(load(own), *near)
    far = [swap_grid(piece, 0, j) for j in (1, 2, 3)]
    up_weight = load(up_weight)
    width = gate_weight.shape[1]
    cut = 896
    low, high = (0, cut), (cut, width)
    theirs_a0, ours_a0, theirs_b0, ours_b0 = project(0, (low, high), piece, far[0], gate_weight, up_weight)
    theirs_a0, theirs_b0 = swap_core(theirs_a0), swap_core(theirs_b0)
    theirs_a1, ours_a1 = project(1, (low,), far[1], far[2], gate_weight, up_weight, after=(ours_a0,))
    theirs_a1 = swap_core(theirs_a1)
    send_a, keep_a = first_sums((ours_a0, ours_a1), (theirs_a0, theirs_a1))
    got_a = swap_z(send_a, 0)
    theirs_b1, ours_b1 = project(1, (high,), far[1], far[2], gate_weight, up_weight, after=(ours_a1,))
    theirs_b1 = swap_core(theirs_b1)
    send_b, keep_b = first_sums((ours_b0, ours_b1), (theirs_b0, theirs_b1), after=(send_a,))
    got_b = swap_z(send_b, 0)
    down_weight = load(down_weight)
    send_a, keep_a = next_sums(got_a, keep_a, after=(send_b,))
    got_a = swap_z(send_a, 1)
    send_b, keep_b = next_sums(got_b, keep_b, after=(send_a,))
    got_b = swap_z(send_b, 1)
    send_a, keep_a = next_sums(got_a, keep_a, after=(send_b, down_weight))
    got_a = swap_z(send_a, 2)
    send_b, keep_b = next_sums(got_b, keep_b, after=(send_a,))
    got_b = swap_z(send_b, 2)
    have_a = activate(got_a, keep_a, after=(send_b,))
    got_a = swap_z(have_a, 2)
    have_b = activate(got_b, keep_b, after=(have_a,))
    got_b = swap_z(have_b, 2)
    for step in (1, 0):
        have_a = join(have_a, got_a, after=(have_b,))
        got_a = swap_z(have_a, step)
        have_b = join(have_b, got_b, after=(have_a,))
        got_b = swap_z(have_b, step)
    hidden_a = assemble(have_a, got_a, after=(have_b,))
    other_a = swap_core(hidden_a)
    hidden_b = assemble(have_b, got_b, after=(hidden_a,))
    other_b = swap_core(hidden_b)
    total = expand(hidden_a, other_a, down_weight)
    terms = expand_rest(hidden_b, other_b, down_weight, total)
    sums = sum_far(terms[0], *[swap_grid(terms[j], 0, j) for j in (2, 1, 3)])
    return sum_near(sums[0], *[swap_grid(sums[k], k, 0) for k in (2, 1, 3)])


def solution(mesh):
    grid = Mesh(mesh.devices.reshape(8, 2, 4, 4), ("z", "core", "x", "y"))
    row, col = ("z", "core"), ("x", "y")
    in_specs = (P(col, row), P(row, col), P(row, col), P(col, row))
    return jax.shard_map(
        on_device, mesh=grid, in_specs=in_specs, out_specs=P(col, row), check_vma=False
    )
```

```python
import jax
import jax.numpy as jnp
from jax import lax
from jax.experimental import pallas as pl
from jax.experimental.pallas import tpu as pltpu
from jax.sharding import Mesh, PartitionSpec as P

BF = jnp.bfloat16
F32 = jnp.float32
VMEM = pl.BlockSpec(memory_space=pltpu.VMEM)
ANY = pl.BlockSpec(memory_space=pl.ANY)
MIB = 2**20

OWNER = (0, 3, 4, 7, 1, 6, 2, 5)
POSITION = sum(t << (4 * z) for t, z in enumerate(OWNER))
STEPS = (1, -1, 3)
FLIP = (0, 2, 1, 3)


def partner(z, step):
    return (z + STEPS[step] * (1 - 2 * (z % 2)) + 8) % 8


def swap_z(v, step):
    pairs = []
    for z in range(8):
        pairs.append((2 * z, 2 * partner(z, step)))
        pairs.append((2 * z + 1, 2 * ((8 - partner((8 - z) % 8, step)) % 8) + 1))
    return lax.ppermute(v, ("z", "core"), pairs)


def swap_core(v):
    return lax.ppermute(v, "core", [(0, 1), (1, 0)])


def swap_grid(v, near, far):
    pairs = []
    for x in range(4):
        for y in range(4):
            pairs.append((4 * x + y, 4 * (x ^ near) + (y ^ far)))
            pairs.append((16 + 4 * x + y, 16 + 4 * (x ^ far) + (y ^ near)))
    return lax.ppermute(v, ("core", "x", "y"), pairs)


def own_z():
    z = lax.axis_index("z")
    return jnp.where(lax.axis_index("core") == 0, z, (8 - z) % 8)


def is_in(z, members):
    return ((sum(1 << m for m in members) >> z) & 1) == 1


def shape(*dims, dtype=BF):
    return jax.ShapeDtypeStruct(dims, dtype)


def call(body, outs, *ins, flops=0, spec=VMEM, scratch=(), limit=16, after=()):
    size = sum(v.size * v.dtype.itemsize for v in (*ins, *outs))
    n = len(ins)
    return pl.pallas_call(
        lambda *refs: body(*refs[len(after) :]),
        out_shape=outs,
        in_specs=[ANY] * len(after) + [spec] * n,
        out_specs=[VMEM] * len(outs),
        scratch_shapes=list(scratch),
        cost_estimate=pl.CostEstimate(flops=1, bytes_accessed=1, transcendentals=0),
        compiler_params=pltpu.CompilerParams(vmem_limit_bytes=limit * MIB),
    )(*after, *ins)


def load(weight):
    def body(source, out, sem):
        copy = pltpu.make_async_copy(source, out, sem)
        copy.start()
        copy.wait()

    sems = [pltpu.SemaphoreType.DMA(())]
    return call(body, [shape(*weight.shape)], weight, spec=ANY, scratch=sems, limit=48)[0]


def join(*parts, after=(), back=False):
    rows = [p.shape[0] for p in parts]

    def body(*refs):
        at = 0
        for ref, n in list(zip(refs, rows))[:: -1 if back else 1]:
            refs[-1][at : at + n] = ref[...]
            at += n

    return call(body, [shape(sum(rows), *parts[0].shape[1:])], *parts, after=after)[0]


def tiles(start, stop, tile):
    return [(at, min(tile, stop - at)) for at in range(start, stop, tile)]


def project(part, columns, first, second, gate_weight, up_weight, after=()):
    _, rows, depth = first.shape
    half = 4 * rows
    widths = [stop - start for start, stop in columns]

    def body(first, second, gate, up, *refs):
        left = refs[-1]
        mine = 2 * (part ^ lax.axis_index("core"))
        for j, ref in enumerate((first, second)):
            for h in range(2):
                at = (2 * j + h) * rows
                left[at : at + rows] = ref[2 - mine + h]
                left[half + at : half + at + rows] = ref[mine + h]
        for n, (start, stop) in enumerate(columns):
            theirs, ours = refs[2 * n : 2 * n + 2]
            for at, size in tiles(start, stop, 256):
                to = slice(at - start, at - start + size)
                for i, weight in enumerate((gate, up)):
                    out = jnp.dot(left[...], weight[:, at : at + size], preferred_element_type=F32)
                    out = out.astype(BF)
                    theirs[:, i, :, to] = out[:half].reshape(4, rows, size)
                    ours[:, i, :, to] = out[half:].reshape(4, rows, size)

    outs = [shape(4, 2, rows, width) for width in widths for _ in range(2)]
    return call(
        body, outs, first, second, gate_weight, up_weight,
        flops=8 * half * depth * sum(widths), scratch=[pltpu.VMEM((2 * half, depth), BF)], after=after,
    )


def first_sums(ours, theirs, after=()):
    _, _, rows, width = ours[0].shape

    def body(o0, o1, t0, t1, send, keep):
        core = lax.axis_index("core")

        def total(t, i):
            p, j, k = t // 4, t // 2 % 2, t % 2
            o, r, s = ((o0, t0, t1), (o1, t1, t0))[p]
            got = jnp.where(core == 0, r[2 * k + j, i], s[2 * k + j, i])
            return o[t % 4, i].astype(F32) + got.astype(F32)

        def fill(kept, sent):
            for n in range(4):
                for i in range(2):
                    send[n, i] = total(sent + n, i).astype(BF)
                    keep[n, i] = total(kept + n, i)

        inside = is_in(own_z(), OWNER[:4])
        pl.when(inside)(lambda: fill(0, 4))
        pl.when(jnp.logical_not(inside))(lambda: fill(4, 0))

    outs = [shape(4, 2, rows, width), shape(4, 2, rows, width, dtype=F32)]
    return call(body, outs, *ours, *theirs, after=after)


def next_sums(got, kept, after=()):
    n, _, rows, width = got.shape
    m = n // 2
    firsts = OWNER[0:2] + OWNER[4:6] if m == 2 else OWNER[::2]

    def body(got, kept, send, keep):
        at = jnp.where(is_in(own_z(), firsts), 0, m)
        for i in range(m):
            send[i] = (got[m - at + i].astype(F32) + kept[m - at + i]).astype(BF)
            keep[i] = got[at + i].astype(F32) + kept[at + i]

    outs = [shape(m, 2, rows, width), shape(m, 2, rows, width, dtype=F32)]
    return call(body, outs, got, kept, after=after)


def activate(got, kept, after=()):
    _, _, rows, width = got.shape

    def body(got, kept, out):
        gate = got[0, 0].astype(F32) + kept[0, 0]
        up = got[0, 1].astype(F32) + kept[0, 1]
        out[0] = (gate / (1 + jnp.exp(-gate)) * up).astype(BF)

    return call(body, [shape(1, rows, width)], got, kept, after=after)[0]


def assemble(sent, got, after=()):
    _, rows, width = sent.shape

    def body(sent, got, out):
        me = own_z()
        for source, ref in ((me, sent), (partner(me, 0), got)):
            near = partner(source, 1)
            for i, owner in enumerate((source, partner(source, 2), near, partner(near, 2))):
                out[(POSITION >> (4 * owner)) & 7] = ref[i]

    return call(body, [shape(8, rows, width)], sent, got, after=after)[0]


def order(own, other, left):
    rows = own.shape[1]
    core = lax.axis_index("core")
    for j in range(4):
        for q in range(4):
            at = (4 * j + q) * rows
            if q < 2:
                left[at : at + rows] = own[2 * j + q]
            else:
                left[at : at + rows] = other[4 * ((j >> 1) ^ 1 ^ core) + 2 * (q - 2) + (j & 1)]


def expand(own, other, weight):
    _, rows, depth = own.shape
    columns = weight.shape[1]

    def body(own, other, weight, total, left):
        order(own, other, left)
        for at, n in tiles(0, columns, 256):
            right = weight[:depth, at : at + n]
            total[:, at : at + n] = jnp.dot(left[...], right, preferred_element_type=F32)

    return call(
        body, [shape(16 * rows, columns, dtype=F32)], own, other, weight,
        flops=32 * rows * depth * columns, scratch=[pltpu.VMEM((16 * rows, depth), BF)],
    )[0]


def expand_rest(own, other, weight, total):
    _, rows, depth = own.shape
    columns = weight.shape[1]
    start = weight.shape[0] - depth

    def body(own, other, weight, total, *refs):
        outs, left = refs[:4], refs[4]
        order(own, other, left)
        for at, n in tiles(0, columns, 256):
            right = weight[start:, at : at + n]
            out = jnp.dot(left[...], right, preferred_element_type=F32) + total[:, at : at + n]
            out = out.astype(BF).reshape(4, 4, rows, n)
            for j in range(4):
                outs[j][:, :, at : at + n] = out[j]

    return call(
        body, [shape(4, rows, columns)] * 4, own, other, weight, total,
        flops=32 * rows * depth * columns, scratch=[pltpu.VMEM((16 * rows, depth), BF)],
    )


def sum_far(*parts):
    _, rows, columns = parts[0].shape

    def body(a, b, c, d, keep, *sends):
        core = lax.axis_index("core")
        for k in range(4):
            low, high = k ^ (2 * core), k ^ 2 ^ (2 * core)
            total = (a[low].astype(F32) + b[low].astype(F32)) + (c[high].astype(F32) + d[high].astype(F32))
            if k == 0:
                keep[...] = total
            else:
                sends[k - 1][...] = total.astype(BF)

    outs = [shape(rows, columns, dtype=F32)] + [shape(rows, columns)] * 3
    return call(body, outs, *parts)


def sum_near(*parts):
    def body(a, b, c, d, out):
        total = (a[...] + b[...].astype(F32)) + (c[...].astype(F32) + d[...].astype(F32))
        out[...] = total.astype(BF)

    return call(body, [shape(*parts[0].shape)], *parts)[0]


def on_device(acts, gate_weight, up_weight, down_weight):
    own = acts[None]
    near = [swap_grid(own, FLIP[k], 0) for k in (3, 2, 1)]
    gate_weight = load(gate_weight)
    piece = join(*near, load(own), back=True)
    far = [swap_grid(piece, 0, FLIP[j]) for j in (1, 2, 3)]
    up_weight = load(up_weight)
    width = gate_weight.shape[1]
    cut = 896
    low, high = (0, cut), (cut, width)
    theirs_a0, ours_a0, theirs_b0, ours_b0 = project(0, (low, high), piece, far[0], gate_weight, up_weight)
    theirs_a0, theirs_b0 = swap_core(theirs_a0), swap_core(theirs_b0)
    theirs_a1, ours_a1 = project(1, (low,), far[1], far[2], gate_weight, up_weight, after=(ours_a0,))
    theirs_a1 = swap_core(theirs_a1)
    send_a, keep_a = first_sums((ours_a0, ours_a1), (theirs_a0, theirs_a1))
    got_a = swap_z(send_a, 0)
    theirs_b1, ours_b1 = project(1, (high,), far[1], far[2], gate_weight, up_weight, after=(ours_a1,))
    theirs_b1 = swap_core(theirs_b1)
    send_b, keep_b = first_sums((ours_b0, ours_b1), (theirs_b0, theirs_b1), after=(send_a,))
    got_b = swap_z(send_b, 0)
    down_weight = load(down_weight)
    send_a, keep_a = next_sums(got_a, keep_a, after=(send_b,))
    got_a = swap_z(send_a, 1)
    send_b, keep_b = next_sums(got_b, keep_b, after=(send_a,))
    got_b = swap_z(send_b, 1)
    send_a, keep_a = next_sums(got_a, keep_a, after=(send_b, down_weight))
    got_a = swap_z(send_a, 2)
    send_b, keep_b = next_sums(got_b, keep_b, after=(send_a,))
    got_b = swap_z(send_b, 2)
    have_a = activate(got_a, keep_a, after=(send_b,))
    got_a = swap_z(have_a, 2)
    have_b = activate(got_b, keep_b, after=(have_a,))
    got_b = swap_z(have_b, 2)
    for step in (1, 0):
        have_a = join(have_a, got_a, after=(have_b,))
        got_a = swap_z(have_a, step)
        have_b = join(have_b, got_b, after=(have_a,))
        got_b = swap_z(have_b, step)
    hidden_a = assemble(have_a, got_a, after=(have_b,))
    other_a = swap_core(hidden_a)
    hidden_b = assemble(have_b, got_b, after=(hidden_a,))
    other_b = swap_core(hidden_b)
    total = expand(hidden_a, other_a, down_weight)
    terms = expand_rest(hidden_b, other_b, down_weight, total)
    sums = sum_far(terms[0], *[swap_grid(terms[j], 0, FLIP[j]) for j in (1, 2, 3)])
    return sum_near(sums[0], *[swap_grid(sums[k], FLIP[k], 0) for k in (1, 2, 3)])


def solution(mesh):
    grid = Mesh(mesh.devices.reshape(8, 2, 4, 4), ("z", "core", "x", "y"))
    row, col = ("z", "core"), ("x", "y")
    in_specs = (P(col, row), P(row, col), P(row, col), P(col, row))
    return jax.shard_map(
        on_device, mesh=grid, in_specs=in_specs, out_specs=P(col, row), check_vma=False
    )
```

```python
import jax
import jax.numpy as jnp
from jax import lax
from jax.experimental import pallas as pl
from jax.experimental.pallas import tpu as pltpu
from jax.sharding import Mesh, PartitionSpec as P

BF = jnp.bfloat16
F32 = jnp.float32
VMEM = pl.BlockSpec(memory_space=pltpu.VMEM)
ANY = pl.BlockSpec(memory_space=pl.ANY)
MIB = 2**20

OWNER = (0, 3, 4, 7, 1, 6, 2, 5)
POSITION = sum(t << (4 * z) for t, z in enumerate(OWNER))
STEPS = (1, -1, 3)
FLIP = (0, 2, 1, 3)


def partner(z, step):
    return (z + STEPS[step] * (1 - 2 * (z % 2)) + 8) % 8


def swap_z(v, step):
    pairs = []
    for z in range(8):
        pairs.append((2 * z, 2 * partner(z, step)))
        pairs.append((2 * z + 1, 2 * ((8 - partner((8 - z) % 8, step)) % 8) + 1))
    return lax.ppermute(v, ("z", "core"), pairs)


def swap_core(v):
    return lax.ppermute(v, "core", [(0, 1), (1, 0)])


def swap_grid(v, near, far):
    pairs = []
    for x in range(4):
        for y in range(4):
            pairs.append((4 * x + y, 4 * (x ^ near) + (y ^ far)))
            pairs.append((16 + 4 * x + y, 16 + 4 * (x ^ far) + (y ^ near)))
    return lax.ppermute(v, ("core", "x", "y"), pairs)


def own_z():
    z = lax.axis_index("z")
    return jnp.where(lax.axis_index("core") == 0, z, (8 - z) % 8)


def is_in(z, members):
    return ((sum(1 << m for m in members) >> z) & 1) == 1


def shape(*dims, dtype=BF):
    return jax.ShapeDtypeStruct(dims, dtype)


def call(body, outs, *ins, flops=0, spec=VMEM, scratch=(), limit=16, after=()):
    size = sum(v.size * v.dtype.itemsize for v in (*ins, *outs))
    n = len(ins)
    return pl.pallas_call(
        lambda *refs: body(*refs[len(after) :]),
        out_shape=outs,
        in_specs=[ANY] * len(after) + [spec] * n,
        out_specs=[VMEM] * len(outs),
        scratch_shapes=list(scratch),
        cost_estimate=pl.CostEstimate(flops=1, bytes_accessed=1, transcendentals=0),
        compiler_params=pltpu.CompilerParams(vmem_limit_bytes=limit * MIB),
    )(*after, *ins)


def load(weight):
    def body(source, out, sem):
        copy = pltpu.make_async_copy(source, out, sem)
        copy.start()
        copy.wait()

    sems = [pltpu.SemaphoreType.DMA(())]
    return call(body, [shape(*weight.shape)], weight, spec=ANY, scratch=sems, limit=48)[0]


def join(*parts, after=(), back=False):
    rows = [p.shape[0] for p in parts]

    def body(*refs):
        at = 0
        for ref, n in list(zip(refs, rows))[:: -1 if back else 1]:
            refs[-1][at : at + n] = ref[...]
            at += n

    return call(body, [shape(sum(rows), *parts[0].shape[1:])], *parts, after=after)[0]


def tiles(start, stop, tile):
    return [(at, min(tile, stop - at)) for at in range(start, stop, tile)]


def project(part, columns, first, second, gate_weight, up_weight, after=()):
    _, rows, depth = first.shape
    half = 4 * rows
    widths = [stop - start for start, stop in columns]

    def body(first, second, gate, up, *refs):
        left = refs[-1]
        mine = 2 * (part ^ lax.axis_index("core"))
        for j, ref in enumerate((first, second)):
            for h in range(2):
                at = (2 * j + h) * rows
                left[at : at + rows] = ref[2 - mine + h]
                left[half + at : half + at + rows] = ref[mine + h]
        for n, (start, stop) in enumerate(columns):
            theirs, ours = refs[2 * n : 2 * n + 2]
            for at, size in tiles(start, stop, 256):
                to = slice(at - start, at - start + size)
                for i, weight in enumerate((gate, up)):
                    out = jnp.dot(left[...], weight[:, at : at + size], preferred_element_type=F32)
                    out = out.astype(BF)
                    theirs[:, i, :, to] = out[:half].reshape(4, rows, size)
                    ours[:, i, :, to] = out[half:].reshape(4, rows, size)

    outs = [shape(4, 2, rows, width) for width in widths for _ in range(2)]
    return call(
        body, outs, first, second, gate_weight, up_weight,
        flops=8 * half * depth * sum(widths), scratch=[pltpu.VMEM((2 * half, depth), BF)], after=after,
    )


def first_sums(ours, theirs, after=()):
    _, _, rows, width = ours[0].shape

    def body(o0, o1, t0, t1, send, keep):
        core = lax.axis_index("core")

        def total(t, i):
            p, j, k = t // 4, t // 2 % 2, t % 2
            o, r, s = ((o0, t0, t1), (o1, t1, t0))[p]
            got = jnp.where(core == 0, r[2 * k + j, i], s[2 * k + j, i])
            return o[t % 4, i].astype(F32) + got.astype(F32)

        def fill(kept, sent):
            for n in range(4):
                for i in range(2):
                    send[n, i] = total(sent + n, i).astype(BF)
                    keep[n, i] = total(kept + n, i)

        inside = is_in(own_z(), OWNER[:4])
        pl.when(inside)(lambda: fill(0, 4))
        pl.when(jnp.logical_not(inside))(lambda: fill(4, 0))

    outs = [shape(4, 2, rows, width), shape(4, 2, rows, width, dtype=F32)]
    return call(body, outs, *ours, *theirs, after=after)


def next_sums(got, kept, after=()):
    n, _, rows, width = got.shape
    m = n // 2
    firsts = OWNER[0:2] + OWNER[4:6] if m == 2 else OWNER[::2]

    def body(got, kept, send, keep):
        at = jnp.where(is_in(own_z(), firsts), 0, m)
        for i in range(m):
            send[i] = (got[m - at + i].astype(F32) + kept[m - at + i]).astype(BF)
            keep[i] = got[at + i].astype(F32) + kept[at + i]

    outs = [shape(m, 2, rows, width), shape(m, 2, rows, width, dtype=F32)]
    return call(body, outs, got, kept, after=after)


def activate(got, kept, after=()):
    _, _, rows, width = got.shape

    def body(got, kept, out):
        gate = got[0, 0].astype(F32) + kept[0, 0]
        up = got[0, 1].astype(F32) + kept[0, 1]
        out[0] = (gate / (1 + jnp.exp(-gate)) * up).astype(BF)

    return call(body, [shape(1, rows, width)], got, kept, after=after)[0]


def assemble(sent, got, after=()):
    _, rows, width = sent.shape

    def body(sent, got, out):
        me = own_z()
        for source, ref in ((me, sent), (partner(me, 0), got)):
            near = partner(source, 1)
            for i, owner in enumerate((source, partner(source, 2), near, partner(near, 2))):
                out[(POSITION >> (4 * owner)) & 7] = ref[i]

    return call(body, [shape(8, rows, width)], sent, got, after=after)[0]


def order(own, other, left):
    rows = own.shape[1]
    core = lax.axis_index("core")
    for j in range(4):
        for q in range(4):
            at = (4 * j + q) * rows
            if q < 2:
                left[at : at + rows] = own[2 * j + q]
            else:
                left[at : at + rows] = other[4 * ((j >> 1) ^ 1 ^ core) + 2 * (q - 2) + (j & 1)]


def expand(own, other, weight):
    _, rows, depth = own.shape
    columns = weight.shape[1]

    def body(own, other, weight, total, left):
        order(own, other, left)
        for at, n in tiles(0, columns, 256):
            right = weight[:depth, at : at + n]
            total[:, at : at + n] = jnp.dot(left[...], right, preferred_element_type=F32)

    return call(
        body, [shape(16 * rows, columns, dtype=F32)], own, other, weight,
        flops=32 * rows * depth * columns, scratch=[pltpu.VMEM((16 * rows, depth), BF)],
    )[0]


def expand_rest(own, other, weight, total):
    _, rows, depth = own.shape
    columns = weight.shape[1]
    start = weight.shape[0] - depth

    def body(own, other, weight, total, *refs):
        outs, left = refs[:4], refs[4]
        order(own, other, left)
        for at, n in tiles(0, columns, 256):
            right = weight[start:, at : at + n]
            out = jnp.dot(left[...], right, preferred_element_type=F32) + total[:, at : at + n]
            out = out.astype(BF).reshape(4, 4, rows, n)
            for j in range(4):
                outs[j][:, :, at : at + n] = out[j]

    return call(
        body, [shape(4, rows, columns)] * 4, own, other, weight, total,
        flops=32 * rows * depth * columns, scratch=[pltpu.VMEM((16 * rows, depth), BF)],
    )


def sum_far(*parts):
    _, rows, columns = parts[0].shape

    def body(a, b, c, d, keep, *sends):
        core = lax.axis_index("core")
        for k in range(4):
            low, high = k ^ (2 * core), k ^ 2 ^ (2 * core)
            total = (a[low].astype(F32) + b[low].astype(F32)) + (c[high].astype(F32) + d[high].astype(F32))
            if k == 0:
                keep[...] = total
            else:
                sends[k - 1][...] = total.astype(BF)

    outs = [shape(rows, columns, dtype=F32)] + [shape(rows, columns)] * 3
    return call(body, outs, *parts)


def sum_near(*parts):
    def body(a, b, c, d, out):
        total = (a[...] + b[...].astype(F32)) + (c[...].astype(F32) + d[...].astype(F32))
        out[...] = total.astype(BF)

    return call(body, [shape(*parts[0].shape)], *parts)[0]


def on_device(acts, gate_weight, up_weight, down_weight):
    own = acts[None]
    near = [swap_grid(own, FLIP[k], 0) for k in (3, 2, 1)]
    gate_weight = load(gate_weight)
    piece = join(*near, load(own), back=True)
    far = [swap_grid(piece, 0, FLIP[j]) for j in (1, 2, 3)]
    up_weight = load(up_weight)
    width = gate_weight.shape[1]
    cut = 896
    low, high = (0, cut), (cut, width)
    theirs_a0, ours_a0, theirs_b0, ours_b0 = project(0, (low, high), piece, far[0], gate_weight, up_weight)
    theirs_a0, theirs_b0 = swap_core(theirs_a0), swap_core(theirs_b0)
    theirs_a1, ours_a1 = project(1, (low,), far[1], far[2], gate_weight, up_weight, after=(ours_a0,))
    theirs_a1 = swap_core(theirs_a1)
    send_a, keep_a = first_sums((ours_a0, ours_a1), (theirs_a0, theirs_a1))
    got_a = swap_z(send_a, 0)
    theirs_b1, ours_b1 = project(1, (high,), far[1], far[2], gate_weight, up_weight, after=(ours_a1,))
    theirs_b1 = swap_core(theirs_b1)
    send_b, keep_b = first_sums((ours_b0, ours_b1), (theirs_b0, theirs_b1), after=(send_a,))
    got_b = swap_z(send_b, 0)
    down_weight = load(down_weight)
    send_a, keep_a = next_sums(got_a, keep_a, after=(send_b,))
    got_a = swap_z(send_a, 1)
    send_b, keep_b = next_sums(got_b, keep_b, after=(send_a,))
    got_b = swap_z(send_b, 1)
    send_a, keep_a = next_sums(got_a, keep_a, after=(send_b, down_weight))
    got_a = swap_z(send_a, 2)
    send_b, keep_b = next_sums(got_b, keep_b, after=(send_a,))
    got_b = swap_z(send_b, 2)
    have_a = activate(got_a, keep_a, after=(send_b,))
    got_a = swap_z(have_a, 2)
    have_b = activate(got_b, keep_b, after=(have_a,))
    got_b = swap_z(have_b, 2)
    for step in (1, 0):
        have_a = join(have_a, got_a, after=(got_b,) if step else (have_b,))
        got_a = swap_z(have_a, step)
        have_b = join(have_b, got_b, after=(have_a,))
        got_b = swap_z(have_b, step)
    hidden_a = assemble(have_a, got_a, after=(have_b,))
    other_a = swap_core(hidden_a)
    hidden_b = assemble(have_b, got_b, after=(hidden_a,))
    other_b = swap_core(hidden_b)
    total = expand(hidden_a, other_a, down_weight)
    terms = expand_rest(hidden_b, other_b, down_weight, total)
    sums = sum_far(terms[0], *[swap_grid(terms[j], 0, FLIP[j]) for j in (1, 2, 3)])
    return sum_near(sums[0], *[swap_grid(sums[k], FLIP[k], 0) for k in (1, 2, 3)])


def solution(mesh):
    grid = Mesh(mesh.devices.reshape(8, 2, 4, 4), ("z", "core", "x", "y"))
    row, col = ("z", "core"), ("x", "y")
    in_specs = (P(col, row), P(row, col), P(row, col), P(col, row))
    return jax.shard_map(
        on_device, mesh=grid, in_specs=in_specs, out_specs=P(col, row), check_vma=False
    )
```
